32 devices in a mesh: gx: 2 (over x), ta: 4 (over y, core), gy: 4 (over z).
Axes of the slice: x: 2, y: 2, z: 4, core: 2. Of those that a mesh axis runs over, the one named last changes fastest.
Arguments:
- initial_field: float32 [22, 20, 5, 128], P('gx', 'gy'), may hold values from -6 to 6
- opening_guess: float32 [4, 22, 20, 5, 128], P('ta', 'gx', 'gy'), may hold values from -6 to 6
- conductivity: float32 [22, 20, 5, 128], P('gx', 'gy'), may hold values from 0.5 to 2
- capacity: float32 [22, 20, 5, 128], P('gx', 'gy'), may hold values from 0.5 to 2
- section_count: int32 [2], P('gx'), may hold values from 3 to 4, as said below
Outputs:
- block_end: float32 [4, 22, 20, 5, 128], P('ta', 'gx', 'gy')
- robin_next: float32 [2, 2, 4, 20, 5, 128], P('gx', None, 'ta', 'gy')
The draws below stay inside these ranges and needn't reach their ends.
Inputs may be any that keep to these rules, and one draw needn't show every extreme that they name: `section_count`: some subdomain takes 3 sections and some takes 4.
All inputs are finite; a program needn't handle non-finite values.
Results may differ from the reference program's by a relative error of at most 0.0003.
Values sent between devices are 32-bit elements; how exact they have to be, the bound alone decides.
A program may use at most 64 MiB of HBM per device.

```python
import math
import jax
import jax.numpy as jnp
import numpy as np
from jax import lax

EZ = 128
STEPS = 1
ITERS = 2
SMIN = 3
SMAX = 4
PX = 11
NX = 22
NY = 20
N_GX = 2
N_TA = 4


def draw_section_count(key, part):
    key = jax.random.fold_in(key, 7)
    first_key, second_key = jax.random.split(key)
    base = jax.random.randint(first_key, (N_GX,), SMIN, SMAX + 1)
    base = base.at[0].set(SMAX).at[1].set(SMIN)
    return jax.random.permutation(second_key, base).astype(jnp.int32)


def level_of(rng, extent, cuts, smallest, top_value):
    level, own = 1.0, jax.random.fold_in(rng, 6)
    for dim, blocks in cuts:
        steps = jnp.exp(jax.random.uniform(jax.random.fold_in(own, dim), (blocks,), jnp.float32, smallest / len(cuts), top_value / len(cuts)))
        level = level * jnp.repeat(steps, extent[dim] // blocks).reshape([-1 if axis == dim else 1 for axis in range(len(extent))])
    return level


def noise(rng, shape, width, limit, cuts=(), held_as=jnp.bfloat16):
    values = width * jax.random.normal(rng, shape, jnp.float32)
    if cuts:
        values = values * level_of(rng, shape, cuts, -0.22, 0.18)
    return jnp.clip(values, -limit, limit).astype(held_as)


def setup_inputs(seed: int = 0) -> dict:
    keys = jax.random.split(jax.random.key(seed), 6)
    return {
        "initial_field": noise(keys[0], (NX, NY, 5, EZ), 1.0, 6.0, ((0, 2), (1, 4)), jnp.float32),
        "opening_guess": noise(keys[1], (N_TA, NX, NY, 5, EZ), 1.0, 6.0, ((0, 4), (1, 2), (2, 4)), jnp.float32),
        "conductivity": jnp.clip(jnp.exp(math.log(2.0) - 1.3862944 * jax.random.uniform(keys[2], (NX, NY, 5, EZ), jnp.float32) ** level_of(keys[2], (NX, NY, 5, EZ), ((0, 2), (1, 4)), -0.2, 0.2)), 0.5, 2.0),
        "capacity": jnp.clip(jnp.exp(math.log(2.0) - 1.3862944 * jax.random.uniform(keys[3], (NX, NY, 5, EZ), jnp.float32) ** level_of(keys[3], (NX, NY, 5, EZ), ((0, 2), (1, 4)), -0.2, 0.2)), 0.5, 2.0),
        "section_count": draw_section_count(jax.random.fold_in(keys[5], 71), 0),
    }


robin_gain = 2.0
kappa_top = 2.0
capacity_low = 0.5
damping = 0.05
highest = lax.Precision.HIGHEST

def gll_tables():
    root_seven = math.sqrt(7.0)
    outer = math.sqrt(1.0 / 3.0 + 2.0 * root_seven / 21.0)
    closer = math.sqrt(1.0 / 3.0 - 2.0 * root_seven / 21.0)
    points = np.array([-1.0, -outer, -closer, closer, outer, 1.0])
    weights = np.array([1.0 / 15.0, (14.0 - root_seven) / 30.0, (14.0 + root_seven) / 30.0, (14.0 + root_seven) / 30.0, (14.0 - root_seven) / 30.0, 1.0 / 15.0])
    products = np.array([np.prod([points[i] - points[k] for k in range(6) if k != i]) for i in range(6)])
    derivative = np.zeros((6, 6))
    for i in range(6):
        for k in range(6):
            if i != k:
                derivative[i, k] = products[i] / (products[k] * (points[i] - points[k]))
    for i in range(6):
        derivative[i, i] = -derivative[i].sum()
    return (points, weights, derivative)

def line_weights(count, closed):
    weights = gll_tables()[1]
    pattern = np.array([weights[i % 5] if i % 5 else 2.0 * weights[0] for i in range(count)])
    if closed:
        pattern[0] = weights[0]
        pattern[-1] = weights[0]
    return pattern

def step_size():
    points, weights, derivative = gll_tables()
    row_sums = np.abs(derivative).sum(axis=1)
    gersh_bound = max((float(np.sum(np.abs(derivative[:, i]) * weights * row_sums) / weights[i]) for i in range(6)))
    spectral = kappa_top / capacity_low * 3.0 * gersh_bound + robin_gain / (capacity_low * weights[0])
    return float(0.8 * 1.93 * SMIN ** 2 / spectral)

def rkc_table(sections):
    section_real = sections.astype(jnp.float32)
    shifted = 1.0 + damping / (section_real * section_real)
    chebyshev = [jnp.ones((), jnp.float32), shifted]
    derivs = [jnp.zeros((), jnp.float32), jnp.ones((), jnp.float32)]
    for section in range(2, SMAX + 1):
        chebyshev.append(2.0 * shifted * chebyshev[-1] - chebyshev[-2])
        derivs.append(2.0 * chebyshev[section - 1] + 2.0 * shifted * derivs[section - 1] - derivs[section - 2])
    cheb_end = jnp.zeros((), jnp.float32)
    slope_end = jnp.zeros((), jnp.float32)
    for section in range(SMIN, SMAX + 1):
        cheb_end = jnp.where(sections == section, chebyshev[section], cheb_end)
        slope_end = jnp.where(sections == section, derivs[section], slope_end)
    spread = cheb_end / slope_end
    coef_mu = [0.0, 0.0] + [2.0 * shifted * chebyshev[j - 1] / chebyshev[j] for j in range(2, SMAX + 1)]
    coef_nu = [0.0, 0.0] + [-chebyshev[j - 2] / chebyshev[j] for j in range(2, SMAX + 1)]
    coef_tilde = [0.0, 0.0] + [2.0 * spread * chebyshev[j - 1] / chebyshev[j] for j in range(2, SMAX + 1)]
    return (spread / shifted, coef_mu, coef_nu, coef_tilde)

def along_first(field):
    element_count = (field.shape[0] - 1) // 5
    leading = field[:-1].reshape((element_count, 5) + field.shape[1:])
    return jnp.concatenate([leading, field[5::5][:, None]], axis=1)

def terms_first(field, tables):
    derivative, quad, kappa_x = (tables['derivative'], tables['quad'], tables['kappa_x'])
    element = along_first(field)
    slopes = jnp.einsum('ab,eb...->ea...', derivative, element, precision=highest)
    flux = slopes * kappa_x * quad[None, :, None, None, None] * tables['scale_x'][None, None]
    returned = jnp.einsum('ab,ea...->eb...', derivative, flux, precision=highest)
    leading = returned[:, :5]
    carried = jnp.concatenate([jnp.zeros_like(returned[:1, 5]), returned[:-1, 5]], axis=0)
    leading = leading.at[:, 0].add(carried)
    element_count = leading.shape[0]
    return jnp.concatenate([leading.reshape((5 * element_count,) + field.shape[1:]), returned[-1:, 5]], axis=0)

def along_second(extended):
    element_count = (extended.shape[1] - 1) // 5
    leading = extended[:, :-1].reshape((extended.shape[0], element_count, 5) + extended.shape[2:])
    return jnp.concatenate([leading, extended[:, 5::5][:, :, None]], axis=2)

def terms_second(extended, kappa_y, tables):
    derivative, quad = (tables['derivative'], tables['quad'])
    element = along_second(extended)
    slopes = jnp.einsum('ab,xeb...->xea...', derivative, element, precision=highest)
    flux = slopes * kappa_y * quad[None, None, :, None, None] * tables['scale_y']
    returned = jnp.einsum('ab,xea...->xeb...', derivative, flux, precision=highest)
    leading = returned[:, :, :5]
    carried = jnp.concatenate([jnp.zeros_like(returned[:, :1, 5]), returned[:, :-1, 5]], axis=1)
    leading = leading.at[:, :, 0].add(carried)
    shape = leading.shape
    interior = leading.reshape((shape[0], shape[1] * 5) + shape[3:])
    return (interior, returned[:, -1, 5])

def along_third(field):
    return jnp.concatenate([field, jnp.roll(field[:, :, :1], -1, axis=3)], axis=2)

def terms_third(field, tables):
    derivative, quad = (tables['derivative'], tables['quad'])
    element = along_third(field)
    slopes = jnp.einsum('ab,xybe->xyae', derivative, element, precision=highest)
    flux = slopes * tables['kappa_z'] * quad[:, None] * tables['scale_z']
    returned = jnp.einsum('ab,xyae->xybe', derivative, flux, precision=highest)
    leading = returned[:, :, :5]
    return leading.at[:, :, 0].add(jnp.roll(returned[:, :, 5], 1, axis=-1))

def build_tables(conductivity, capacity):
    points, weights, derivative = gll_tables()
    weight_x = jnp.asarray(line_weights(conductivity.shape[0], True), jnp.float32)
    weight_y = jnp.asarray(line_weights(conductivity.shape[1], False), jnp.float32)
    weight_z = jnp.asarray(line_weights(5, False), jnp.float32)
    return {'derivative': jnp.asarray(derivative, jnp.float32), 'quad': jnp.asarray(weights, jnp.float32), 'kappa_x': along_first(conductivity), 'kappa_z': along_third(conductivity), 'scale_x': (weight_y[:, None] * weight_z[None, :])[:, :, None], 'scale_y': (weight_x[:, None] * weight_z[None, :])[:, None, None, :, None], 'scale_z': (weight_x[:, None] * weight_y[None, :])[:, :, None, None], 'face_weight': (weight_y[:, None] * weight_z[None, :])[:, :, None], 'lumped': capacity * weight_x[:, None, None, None] * weight_y[None, :, None, None] * weight_z[None, None, :, None]}

def rate(field, second_value, left_data, right_data, tables):
    summed = terms_first(field, tables) + second_value + terms_third(field, tables)
    change = -summed
    face_weight = tables['face_weight']
    change = change.at[0].add(face_weight * (left_data - robin_gain * field[0]))
    change = change.at[-1].add(face_weight * (right_data - robin_gain * field[-1]))
    return change / tables['lumped']

def advance(opening, left_hist, right_hist, sections, second_terms, tables):
    step_len = step_size()
    opening_coef, coef_mu, coef_nu, coef_tilde = rkc_table(sections)
    field = opening
    left_trace = []
    right_trace = []
    for step in range(STEPS):
        left_trace.append(field[0])
        right_trace.append(field[-1])
        earlier = field
        current = field + opening_coef * step_len * rate(field, second_terms(field), left_hist[step], right_hist[step], tables)
        for section in range(2, SMAX + 1):
            updated = coef_mu[section] * current + coef_nu[section] * earlier + coef_tilde[section] * step_len * rate(current, second_terms(current), left_hist[step], right_hist[step], tables)
            active = section <= sections
            earlier, current = (jnp.where(active, current, earlier), jnp.where(active, updated, current))
        field = current
    return (field, jnp.stack(left_trace), jnp.stack(right_trace))

def solve_one(opening, left_hist, right_hist, sections, conductivity, capacity):
    tables = build_tables(conductivity, capacity)
    kappa_y = along_second(jnp.concatenate([conductivity, conductivity[:, :1]], axis=1))

    def second_terms(field):
        interior, spill = terms_second(jnp.concatenate([field, field[:, :1]], axis=1), kappa_y, tables)
        return interior.at[:, 0].add(spill)
    return advance(opening, left_hist, right_hist, sections, second_terms, tables)

def reference(initial_field, opening_guess, conductivity, capacity, section_count):
    sub_shape = (N_GX, PX) + initial_field.shape[1:]
    initial_sub = initial_field.reshape(sub_shape)
    guess_sub = opening_guess.reshape((N_TA,) + sub_shape)
    conductivity_sub = conductivity.reshape(sub_shape)
    capacity_sub = capacity.reshape(sub_shape)
    inner_map = jax.vmap(solve_one, in_axes=(0, 0, 0, 0, 0, 0))
    outer_map = jax.vmap(inner_map, in_axes=(0, 0, 0, None, None, None))
    hist_shape = (N_TA, N_GX, STEPS) + initial_field.shape[1:]
    left_hist = jnp.zeros(hist_shape, jnp.float32)
    right_hist = jnp.zeros(hist_shape, jnp.float32)
    opening = jnp.concatenate([initial_sub[None], guess_sub[1:]], axis=0)
    finish = opening
    for sweep in range(ITERS):
        finish, left_trace, right_trace = outer_map(opening, left_hist, right_hist, section_count, conductivity_sub, capacity_sub)
        send_left = 2.0 * robin_gain * left_trace - left_hist
        send_right = 2.0 * robin_gain * right_trace - right_hist
        left_hist = jnp.concatenate([jnp.zeros_like(send_right[:, :1]), send_right[:, :-1]], axis=1)
        right_hist = jnp.concatenate([send_left[:, 1:], jnp.zeros_like(send_left[:, :1])], axis=1)
        if sweep + 1 < ITERS:
            opening = jnp.concatenate([initial_sub[None], finish[:-1]], axis=0)
    block_end = finish.reshape((N_TA, N_GX * PX) + initial_field.shape[1:])
    robin = jnp.stack([left_hist, right_hist], axis=2)
    robin = jnp.transpose(robin, (1, 2, 0, 3, 4, 5, 6))
    robin_next = robin.reshape((N_GX, 2, N_TA * STEPS) + initial_field.shape[1:])
    return (block_end, robin_next)
```

```python
import functools
import math

import jax
import jax.numpy as jnp
import ml_dtypes
import numpy as np
from jax import lax
from jax.experimental import pallas as pl
from jax.experimental.pallas import tpu as pltpu
from jax.sharding import PartitionSpec as P

ITERS = 2
SMIN = 3
SMAX = 4
LANES = 128
PLANES = 6
MESH = pl.DeviceIdType.MESH

robin_gain = 2.0
kappa_top = 2.0
capacity_low = 0.5
damping = 0.05


def gll_tables():
    root_seven = math.sqrt(7.0)
    outer = math.sqrt(1.0 / 3.0 + 2.0 * root_seven / 21.0)
    closer = math.sqrt(1.0 / 3.0 - 2.0 * root_seven / 21.0)
    points = np.array([-1.0, -outer, -closer, closer, outer, 1.0])
    low, high = (14.0 - root_seven) / 30.0, (14.0 + root_seven) / 30.0
    weights = np.array([1.0 / 15.0, low, high, high, low, 1.0 / 15.0])
    products = np.array(
        [np.prod([points[i] - points[k] for k in range(6) if k != i]) for i in range(6)]
    )
    derivative = np.zeros((6, 6))
    for i in range(6):
        for k in range(6):
            if i != k:
                derivative[i, k] = products[i] / (products[k] * (points[i] - points[k]))
    for i in range(6):
        derivative[i, i] = -derivative[i].sum()
    return (points, weights, derivative)


def line_weights(count, closed):
    weights = gll_tables()[1]
    pattern = np.array([weights[i % 5] if i % 5 else 2.0 * weights[0] for i in range(count)])
    if closed:
        pattern[0] = weights[0]
        pattern[-1] = weights[0]
    return pattern


def step_size():
    points, weights, derivative = gll_tables()
    row_sums = np.abs(derivative).sum(axis=1)
    gersh_bound = max(
        float(np.sum(np.abs(derivative[:, i]) * weights * row_sums) / weights[i]) for i in range(6)
    )
    spectral = kappa_top / capacity_low * 3.0 * gersh_bound + robin_gain / (
        capacity_low * weights[0]
    )
    return float(0.8 * 1.93 * SMIN**2 / spectral)


def rkc_table(sections):
    shifted = 1.0 + damping / sections**2
    cheb, derivs = [1.0, shifted], [0.0, 1.0]
    for j in range(2, SMAX + 1):
        cheb.append(2.0 * shifted * cheb[-1] - cheb[-2])
        derivs.append(2.0 * cheb[j - 1] + 2.0 * shifted * derivs[j - 1] - derivs[j - 2])
    spread = cheb[sections] / derivs[sections]
    rows = [(1.0, 0.0, spread / shifted)]
    for j in range(2, SMAX + 1):
        if j <= sections:
            rows.append(
                (
                    2.0 * shifted * cheb[j - 1] / cheb[j],
                    -cheb[j - 2] / cheb[j],
                    2.0 * spread * cheb[j - 1] / cheb[j],
                )
            )
        else:
            rows.append((1.0, 0.0, 0.0))
    return np.array(rows)


def stacked(matrix):
    matrix = matrix.astype(np.float32)
    high = matrix.astype(ml_dtypes.bfloat16)
    low = (matrix - high.astype(np.float32)).astype(ml_dtypes.bfloat16)
    return np.concatenate([high, high, low], axis=1)


def row_order(px):
    inner = list(range(1, px - 1))
    first, second, third = inner[:3], inner[3:6], inner[6:]
    rows = [(0, q) for q in range(5)] + [(x, 0) for x in first]
    rows += [(px - 1, q) for q in range(5)] + [(x, 0) for x in second]
    rows += [(x, 0) for x in third]
    rows += [(x, q) for x in inner for q in range(1, 5)]
    while len(rows) % 8:
        rows.append((1, 1))
    return rows


LEAD = 24


def constants(px):
    points, quad, deriv = gll_tables()
    wx, wz = line_weights(px, True), line_weights(5, False)
    rows = row_order(px)
    count = len(rows)
    place = {}
    for r, node in enumerate(rows):
        place.setdefault(node, r)
    elements = (px - 1) // 5
    slope_rows = elements * 30 + px * 6
    padded = -(-slope_rows // 16) * 16
    slope = np.zeros((padded, count + LEAD))
    spread = np.zeros((padded, count + LEAD))
    r = 0
    for e in range(elements):
        for a in range(6):
            for q in range(5):
                for b in range(6):
                    slope[r, place[5 * e + b, q]] = deriv[a, b]
                spread[r, place[5 * e + a, q]] = quad[a] * wz[q]
                r += 1
    for x in range(px):
        for a in range(6):
            for b in range(5):
                slope[r, place[x, b]] = deriv[a, b]
            slope[r, count + place[x, 0]] = deriv[a, 5]
            source = place[x, a] if a < 5 else count + place[x, 0]
            spread[r, source] = quad[a] * wx[x]
            r += 1
    gather = np.zeros((count, px * 8), np.float32)
    scatter = np.zeros((px * 8, count), np.float32)
    for r, (x, q) in enumerate(rows):
        gather[r, 8 * x + q] = 1.0
    for (x, q), r in place.items():
        scatter[8 * x + q, r] = 1.0
    ones = np.ones((1, LANES))
    weight = np.array([wx[x] * wz[q] for x, q in rows])[:, None] * ones
    face = np.zeros((16, 1))
    face[0:5, 0] = wz
    face[8:13, 0] = wz
    table = np.stack([rkc_table(s).reshape(-1) for s in range(SMIN, SMAX + 1)])
    f32 = np.float32
    return (
        stacked(slope),
        stacked(slope.T),
        stacked(spread),
        gather,
        scatter,
        weight.astype(f32),
        (face * ones).astype(f32),
        table.astype(f32),
    )


def halves(value):
    high = value.astype(jnp.bfloat16)
    low = (value - high.astype(jnp.float32)).astype(jnp.bfloat16)
    return jnp.concatenate([high, low, high], axis=0)


def product(matrix, value):
    return jnp.dot(matrix, halves(value), preferred_element_type=jnp.float32)


def exact(matrix, value):
    return jnp.dot(
        matrix, value, preferred_element_type=jnp.float32, precision=lax.Precision.HIGHEST
    )


def plane(b):
    return slice(LANES * b, LANES * (b + 1))


def rolled(value, shift):
    parts = value.shape[1] // LANES
    return jnp.concatenate(
        [pltpu.roll(value[:, plane(b)], shift % LANES, 1) for b in range(parts)], axis=1
    )


def extended(value):
    return jnp.concatenate([value, rolled(value[:LEAD], -1)], axis=0)


def padded_rows(value):
    zeros = jnp.zeros((value.shape[0], 3, LANES), value.dtype)
    return jnp.concatenate([value, zeros], axis=1).reshape(8 * value.shape[0], LANES)


def kernel(
    sizes,
    step_len,
    init_ref, guess_ref, cond_ref, cap_ref, sec_ref,
    slope_ref, back_ref, spread_ref, gather_ref, scatter_ref, weight_ref, face_ref, table_ref,
    end_ref, robin_ref,
    field, opened, arrived, inv, flux_x, flux_y, part, raw_open, raw_in,
    send_y, recv_y, faces_in, faces_out, faces_next, hist, drive,
    raw_send, raw_recv, y_send, y_recv, f_send, f_recv, t_send, t_recv,
):
    n_gx, n_ta, n_gy = sizes
    quad, deriv = gll_tables()[1:]
    deriv = [[float(v) for v in row] for row in deriv]
    wy = [float(2.0 * quad[0])] + [float(quad[b]) for b in range(1, 5)] + [float(2.0 * quad[0])]
    gx, ta, gy = lax.axis_index("gx"), lax.axis_index("ta"), lax.axis_index("gy")
    ahead, behind = lax.rem(gy + 1, n_gy), lax.rem(gy + n_gy - 1, n_gy)
    has_left, has_right = gx > 0, gx < n_gx - 1
    has_before, has_after = ta > 0, ta < n_ta - 1

    barrier = pltpu.get_barrier_semaphore()

    def greet(target):
        pl.semaphore_signal(barrier, inc=1, device_id=target, device_id_type=MESH)

    greet({"gy": ahead})
    greet({"gy": behind})
    for there, name, index in (
        (has_left, "gx", gx - 1),
        (has_right, "gx", gx + 1),
        (has_before, "ta", ta - 1),
        (has_after, "ta", ta + 1),
    ):
        pl.when(there)(functools.partial(greet, {name: index}))

    first = ta == 0
    px = init_ref.shape[0]
    raw_open[...] = jnp.where(first, init_ref[:, 0], guess_ref[0, :, 0])
    expected = 2
    for there in (has_left, has_right, has_before, has_after):
        expected = expected + there.astype(jnp.int32)
    pl.semaphore_wait(barrier, expected)

    raws = []
    for k, source in enumerate((raw_open, cond_ref.at[:, 0], cap_ref.at[:, 0])):
        copy = pltpu.make_async_remote_copy(
            src_ref=source, dst_ref=raw_in.at[k], send_sem=raw_send.at[k],
            recv_sem=raw_recv.at[k], device_id={"gy": behind}, device_id_type=MESH,
        )
        copy.start()
        raws.append(copy)

    gather = gather_ref[...]
    weight = weight_ref[...]

    def packed(ref):
        wide = jnp.concatenate([padded_rows(ref[:, b]) for b in range(5)], axis=1)
        return exact(gather, wide)

    def set_tables(first_plane, count, kappa, capacity):
        spread_out = product(spread_ref[...], extended(kappa))
        for i in range(count):
            b = first_plane + i
            flux_x[:, plane(b)] = spread_out[:, plane(i)] * wy[b]
            flux_y[:, plane(b)] = kappa[:, plane(i)] * weight * float(quad[b])
            inv[:, plane(b)] = (step_len / wy[b]) / (capacity[:, plane(i)] * weight)

    own = slice(0, 5 * LANES)
    wide = jnp.concatenate(
        [
            padded_rows(jnp.where(first, init_ref[:, b], guess_ref[0, :, b]))
            for b in range(5)
        ],
        axis=1,
    )
    opened[:, own] = exact(gather, wide)
    set_tables(0, 5, packed(cond_ref), packed(cap_ref))
    for copy in raws:
        copy.wait()
    last = [exact(gather, padded_rows(raw_in[k])) for k in range(3)]
    opened[:, plane(5)] = last[0]
    set_tables(5, 1, last[1], last[2])

    field[0] = opened[...]
    field[1] = opened[...]
    faces_out[0] = opened[0:8]
    faces_out[1] = opened[8:16]
    drive[...] = jnp.zeros_like(drive)

    def face_copies(source, target, base):
        to_left = pltpu.make_async_remote_copy(
            src_ref=source.at[0], dst_ref=target.at[1], send_sem=f_send.at[base],
            recv_sem=f_recv.at[base + 1], device_id={"gx": gx - 1}, device_id_type=MESH,
        )
        to_right = pltpu.make_async_remote_copy(
            src_ref=source.at[1], dst_ref=target.at[0], send_sem=f_send.at[base + 1],
            recv_sem=f_recv.at[base], device_id={"gx": gx + 1}, device_id_type=MESH,
        )
        return to_left, to_right

    def start_faces(copies):
        pl.when(has_left)(copies[0].start)
        pl.when(has_right)(copies[1].start)

    def wait_faces(copies):
        @pl.when(has_left)
        def _():
            copies[0].wait_send()
            copies[1].wait_recv()

        @pl.when(has_right)
        def _():
            copies[1].wait_send()
            copies[0].wait_recv()

    faces = face_copies(faces_out, faces_in, 0)
    start_faces(faces)

    sections = sec_ref[0]
    face = face_ref[...]

    def coefficient(j, k):
        value = table_ref[0, 3 * j + k]
        for s in range(1, SMAX - SMIN + 1):
            value = jnp.where(sections == SMIN + s, table_ref[s, 3 * j + k], value)
        return value

    def combine(terms):
        total = terms[0]
        for term in terms[1:]:
            total = total + term
        return total

    def stage(sweep, j, carry):
        n = sweep * SMAX + j
        now = lax.rem(j, 2)
        later = 1 - now
        mu, nu, tilde = (coefficient(j, k) for k in range(3))
        u = [field[now, :, plane(b)] for b in range(PLANES)]
        flux = [
            flux_y[:, plane(a)] * combine([deriv[a][b] * u[b] for b in range(PLANES)])
            for a in range(PLANES)
        ]

        def returned(b):
            return combine([deriv[a][b] * flux[a] for a in range(PLANES)])

        edge = (returned(0), returned(5))
        copies = []
        for side, target in ((0, behind), (1, ahead)):
            send_y[n, side] = edge[side]
            copy = pltpu.make_async_remote_copy(
                src_ref=send_y.at[n, side], dst_ref=recv_y.at[n, 1 - side],
                send_sem=y_send.at[n, side], recv_sem=y_recv.at[n, 1 - side],
                device_id={"gy": target}, device_id_type=MESH,
            )
            copy.start()
            copies.append(copy)

        whole = field[now]
        slopes = product(slope_ref[...], extended(whole))
        back = product(back_ref[...], slopes * flux_x[...])
        count = whole.shape[0]
        wrapped = rolled(back[count:], 1)

        def assembled(b, second):
            value = back[:count, plane(b)] + second
            lead = value[:LEAD] + wrapped[:, plane(b)]
            top = lead[:16] + face * (robin_gain * wy[b]) * u[b][:16] - drive[:, plane(b)]
            return jnp.concatenate([top, lead[16:], value[LEAD:]], axis=0)

        for b in range(1, 5):
            total = assembled(b, returned(b))
            field[later, :, plane(b)] = (
                mu * u[b] + nu * field[later, :, plane(b)] - tilde * (inv[:, plane(b)] * total)
            )
        for side, b in ((0, 0), (1, 5)):
            total = assembled(b, edge[side])
            part[side] = (
                mu * u[b] + nu * field[later, :, plane(b)] - tilde * (inv[:, plane(b)] * total)
            )
        copies[0].wait()
        copies[1].wait()
        for side, b in ((0, 0), (1, 5)):
            field[later, :, plane(b)] = part[side] - tilde * (inv[:, plane(b)] * recv_y[n, side])
        return carry

    lax.fori_loop(0, SMAX, functools.partial(stage, 0), 0)

    onward = pltpu.make_async_remote_copy(
        src_ref=field.at[SMAX % 2], dst_ref=arrived, send_sem=t_send, recv_sem=t_recv,
        device_id={"ta": ta + 1}, device_id_type=MESH,
    )
    pl.when(has_after)(onward.start)

    wait_faces(faces)
    for side, there in ((0, has_left), (1, has_right)):
        @pl.when(there)
        def _():
            hist[side] = (2.0 * robin_gain) * faces_in[side]

        @pl.when(jnp.logical_not(there))
        def _():
            hist[side] = jnp.zeros(hist.shape[1:], jnp.float32)
    for b in range(PLANES):
        for side in range(2):
            rows = slice(8 * side, 8 * side + 8)
            drive[rows, plane(b)] = face[rows] * wy[b] * hist[side, :, plane(b)]

    pl.when(has_after)(onward.wait_send)

    @pl.when(has_before)
    def _():
        onward.wait_recv()
        field[0] = arrived[...]
        field[1] = arrived[...]

    @pl.when(first)
    def _():
        field[0] = opened[...]
        field[1] = opened[...]

    for side in range(2):
        faces_next[0, side] = (2.0 * robin_gain) * field[
            0, 8 * side : 8 * side + 8, own
        ] - hist[side, :, own]
    faces = face_copies(faces_next.at[0], faces_next.at[1], 2)
    start_faces(faces)

    lax.fori_loop(0, SMAX, functools.partial(stage, 1), 0)

    wide = exact(scatter_ref[...], field[SMAX % 2, :, own])
    for b in range(5):
        end_ref[0, :, b] = wide[:, plane(b)].reshape(px, 8, LANES)[:, :5]
    wait_faces(faces)
    for side, there in ((0, has_left), (1, has_right)):
        @pl.when(there)
        def _():
            for b in range(5):
                robin_ref[0, side, 0, b] = faces_next[1, side, 0:5, plane(b)]

        @pl.when(jnp.logical_not(there))
        def _():
            robin_ref[0, side, 0] = jnp.zeros(robin_ref.shape[3:], jnp.float32)


def solution(mesh):
    sizes = tuple(mesh.shape[name] for name in ("gx", "ta", "gy"))

    def local(initial_field, opening_guess, conductivity, capacity, section_count):
        px = initial_field.shape[0]
        tables = constants(px)
        count = len(row_order(px))
        slope_rows = tables[0].shape[0]
        total = PLANES * LANES
        f32 = jnp.float32
        vmem = pl.BlockSpec(memory_space=pltpu.VMEM)
        smem = pl.BlockSpec(memory_space=pltpu.SMEM)
        stages = ITERS * SMAX
        dma = pltpu.SemaphoreType.DMA
        return pl.pallas_call(
            functools.partial(kernel, sizes, step_size()),
            out_shape=(
                jax.ShapeDtypeStruct(opening_guess.shape, f32),
                jax.ShapeDtypeStruct((1, 2, 1) + initial_field.shape[1:], f32),
            ),
            in_specs=[vmem] * 4 + [smem] + [vmem] * 7 + [smem],
            out_specs=(vmem, vmem),
            scratch_shapes=[
                pltpu.VMEM((2, count, total), f32),
                pltpu.VMEM((count, total), f32),
                pltpu.VMEM((count, total), f32),
                pltpu.VMEM((count, total), f32),
                pltpu.VMEM((slope_rows, total), f32),
                pltpu.VMEM((count, total), f32),
                pltpu.VMEM((2, count, LANES), f32),
                pltpu.VMEM((px, 5, LANES), f32),
                pltpu.VMEM((3, px, 5, LANES), f32),
                pltpu.VMEM((stages, 2, count, LANES), f32),
                pltpu.VMEM((stages, 2, count, LANES), f32),
                pltpu.VMEM((2, 8, total), f32),
                pltpu.VMEM((2, 8, total), f32),
                pltpu.VMEM((2, 2, 8, 5 * LANES), f32),
                pltpu.VMEM((2, 8, total), f32),
                pltpu.VMEM((16, total), f32),
                dma((3,)), dma((3,)),
                dma((stages, 2)), dma((stages, 2)),
                dma((4,)), dma((4,)),
                dma, dma,
            ],
            compiler_params=pltpu.CompilerParams(
                collective_id=0, has_side_effects=True, vmem_limit_bytes=32 * 1024 * 1024
            ),
        )(
            initial_field, opening_guess, conductivity, capacity, section_count,
            *[jnp.asarray(t) for t in tables],
        )

    return jax.shard_map(
        local,
        mesh=mesh,
        in_specs=(
            P("gx", "gy", None, None),
            P("ta", "gx", "gy", None, None),
            P("gx", "gy", None, None),
            P("gx", "gy", None, None),
            P("gx"),
        ),
        out_specs=(P("ta", "gx", "gy", None, None), P("gx", None, "ta", "gy", None, None)),
        check_vma=False,
    )
```

```python
import functools
import math

import jax
import jax.numpy as jnp
import ml_dtypes
import numpy as np
from jax import lax
from jax.experimental import pallas as pl
from jax.experimental.pallas import tpu as pltpu
from jax.sharding import PartitionSpec as P

ITERS = 2
SMIN = 3
SMAX = 4
LANES = 128
MESH = pl.DeviceIdType.MESH

robin_gain = 2.0
kappa_top = 2.0
capacity_low = 0.5
damping = 0.05


def gll_tables():
    root_seven = math.sqrt(7.0)
    outer = math.sqrt(1.0 / 3.0 + 2.0 * root_seven / 21.0)
    closer = math.sqrt(1.0 / 3.0 - 2.0 * root_seven / 21.0)
    points = np.array([-1.0, -outer, -closer, closer, outer, 1.0])
    low, high = (14.0 - root_seven) / 30.0, (14.0 + root_seven) / 30.0
    weights = np.array([1.0 / 15.0, low, high, high, low, 1.0 / 15.0])
    products = np.array(
        [np.prod([points[i] - points[k] for k in range(6) if k != i]) for i in range(6)]
    )
    derivative = np.zeros((6, 6))
    for i in range(6):
        for k in range(6):
            if i != k:
                derivative[i, k] = products[i] / (products[k] * (points[i] - points[k]))
    for i in range(6):
        derivative[i, i] = -derivative[i].sum()
    return (points, weights, derivative)


def line_weights(count, closed):
    weights = gll_tables()[1]
    pattern = np.array([weights[i % 5] if i % 5 else 2.0 * weights[0] for i in range(count)])
    if closed:
        pattern[0] = weights[0]
        pattern[-1] = weights[0]
    return pattern


def step_size():
    points, weights, derivative = gll_tables()
    row_sums = np.abs(derivative).sum(axis=1)
    gersh_bound = max(
        float(np.sum(np.abs(derivative[:, i]) * weights * row_sums) / weights[i]) for i in range(6)
    )
    spectral = kappa_top / capacity_low * 3.0 * gersh_bound + robin_gain / (
        capacity_low * weights[0]
    )
    return float(0.8 * 1.93 * SMIN**2 / spectral)


def rkc_table(sections):
    shifted = 1.0 + damping / sections**2
    cheb, derivs = [1.0, shifted], [0.0, 1.0]
    for j in range(2, SMAX + 1):
        cheb.append(2.0 * shifted * cheb[-1] - cheb[-2])
        derivs.append(2.0 * cheb[j - 1] + 2.0 * shifted * derivs[j - 1] - derivs[j - 2])
    spread = cheb[sections] / derivs[sections]
    rows = [(1.0, 0.0, spread / shifted)]
    for j in range(2, SMAX + 1):
        if j <= sections:
            rows.append(
                (
                    2.0 * shifted * cheb[j - 1] / cheb[j],
                    -cheb[j - 2] / cheb[j],
                    2.0 * spread * cheb[j - 1] / cheb[j],
                )
            )
        else:
            rows.append((1.0, 0.0, 0.0))
    return np.array(rows)


def stacked(matrix):
    matrix = matrix.astype(np.float32)
    high = matrix.astype(ml_dtypes.bfloat16)
    low = (matrix - high.astype(np.float32)).astype(ml_dtypes.bfloat16)
    return np.concatenate([high, high, low], axis=1)


def row_order(px):
    inner = list(range(1, px - 1))
    first, second, third = inner[:3], inner[3:6], inner[6:]
    rows = [(0, q) for q in range(5)] + [(x, 0) for x in first]
    rows += [(px - 1, q) for q in range(5)] + [(x, 0) for x in second]
    rows += [(x, 0) for x in third]
    rows += [(x, q) for x in inner for q in range(1, 5)]
    while len(rows) % 8:
        rows.append((1, 1))
    return rows


LEAD = 24


def constants(px):
    points, quad, deriv = gll_tables()
    wx, wz = line_weights(px, True), line_weights(5, False)
    rows = row_order(px)
    count = len(rows)
    place = {}
    for r, node in enumerate(rows):
        place.setdefault(node, r)
    elements = (px - 1) // 5
    slope_rows = elements * 30 + px * 6
    padded = -(-slope_rows // 16) * 16
    slope = np.zeros((padded, count + LEAD))
    spread = np.zeros((padded, count + LEAD))
    r = 0
    for e in range(elements):
        for a in range(6):
            for q in range(5):
                for b in range(6):
                    slope[r, place[5 * e + b, q]] = deriv[a, b]
                spread[r, place[5 * e + a, q]] = quad[a] * wz[q]
                r += 1
    for x in range(px):
        for a in range(6):
            for b in range(5):
                slope[r, place[x, b]] = deriv[a, b]
            slope[r, count + place[x, 0]] = deriv[a, 5]
            source = place[x, a] if a < 5 else count + place[x, 0]
            spread[r, source] = quad[a] * wx[x]
            r += 1
    high = -(-px // 8) * 8
    gather = np.zeros((count, 5 * high), np.float32)
    scatter = np.zeros((px * 8, count), np.float32)
    for r, (x, q) in enumerate(rows):
        gather[r, high * q + x] = 1.0
    for (x, q), r in place.items():
        scatter[8 * x + q, r] = 1.0
    ones = np.ones((1, LANES))
    weight = np.array([wx[x] * wz[q] for x, q in rows])[:, None] * ones
    face = np.zeros((16, 1))
    face[0:5, 0] = wz
    face[8:13, 0] = wz
    table = np.stack([rkc_table(s).reshape(-1) for s in range(SMIN, SMAX + 1)])
    f32 = np.float32
    return (
        stacked(slope),
        stacked(slope.T),
        stacked(spread),
        gather,
        scatter,
        weight.astype(f32),
        (face * ones).astype(f32),
        table.astype(f32),
    )


def halves(value):
    high = value.astype(jnp.bfloat16)
    low = (value - high.astype(jnp.float32)).astype(jnp.bfloat16)
    return jnp.concatenate([high, low, high], axis=0)


def product(matrix, value):
    return jnp.dot(matrix, halves(value), preferred_element_type=jnp.float32)


def exact(matrix, value):
    return jnp.dot(
        matrix, value, preferred_element_type=jnp.float32, precision=lax.Precision.HIGHEST
    )


def plane(b):
    return slice(LANES * b, LANES * (b + 1))


def rolled(value, shift):
    parts = value.shape[1] // LANES
    return jnp.concatenate(
        [pltpu.roll(value[:, plane(b)], shift % LANES, 1) for b in range(parts)], axis=1
    )


def extended(value):
    return jnp.concatenate([value, rolled(value[:LEAD], -1)], axis=0)


def wide_rows(ref):
    px = ref.shape[2]
    extra = -px % 8
    zeros = jnp.zeros((5, extra, LANES), jnp.float32)
    return [
        jnp.concatenate([ref[b], zeros], axis=1).reshape(5 * (px + extra), LANES)
        for b in range(5)
    ]


def kernel(
    sizes,
    step_len,
    init_ref, guess_ref, cond_ref, cap_ref, sec_ref,
    slope_ref, back_ref, spread_ref, gather_ref, scatter_ref, weight_ref, face_ref, table_ref,
    end_ref, robin_ref,
    field, inputs, inv, flux_x, flux_y, y_terms, spill, packs, ends_in,
    faces_out, faces_in, robin_out, robin_in, hist, drive,
    in_send, in_recv, f_send, f_recv, r_send, r_recv, e_send, e_recv,
):
    n_gx, n_ta, n_gy = sizes
    quad, deriv = gll_tables()[1:]
    deriv = [[float(v) for v in row] for row in deriv]
    wy = [float(2.0 * quad[0])] + [float(quad[b]) for b in range(1, 5)]
    gx, ta, gy = lax.axis_index("gx"), lax.axis_index("ta"), lax.axis_index("gy")
    after, before = lax.rem(ta + 1, n_ta), lax.rem(ta + n_ta - 1, n_ta)
    low_hub, hubs = (n_gy - 1) // 2, 1 if n_gy == 1 else 2

    def hub_of(block):
        return low_hub + lax.rem(block, hubs)

    hub, hub_before = hub_of(ta), hub_of(before)
    is_hub = gy == hub
    sides = ((gx > 0, gx - 1), (gx < n_gx - 1, gx + 1))
    px = init_ref.shape[2]

    barrier = pltpu.get_barrier_semaphore()

    def greet(x, t, y):
        pl.semaphore_signal(
            barrier, inc=1, device_id={"gx": x, "ta": t, "gy": y}, device_id_type=MESH
        )

    neighbours = sides[0][0].astype(jnp.int32) + sides[1][0].astype(jnp.int32)
    greet(gx, before, hub_before)
    for there, x in sides:
        pl.when(there)(functools.partial(greet, x, before, hub_before))
    pl.when(jnp.logical_not(is_hub))(functools.partial(greet, gx, ta, hub))

    @pl.when(is_hub)
    def _():
        for p in range(n_gy):
            pl.when(gy != p)(functools.partial(greet, gx, ta, p))
            greet(gx, after, p)
            for there, x in sides:
                pl.when(there)(functools.partial(greet, x, after, p))

    gather = gather_ref[...]
    first = ta == 0
    starts_first = jnp.logical_or(first, ta == n_ta - 1)
    fresh, guess = wide_rows(init_ref), wide_rows(guess_ref)

    def chosen(there):
        return jnp.concatenate(
            [jnp.where(there, fresh[b], guess[b]) for b in range(5)], axis=1
        )

    packs[0] = exact(gather, jnp.concatenate(wide_rows(cond_ref), axis=1))
    packs[1] = exact(gather, jnp.concatenate(wide_rows(cap_ref), axis=1))
    packs[2] = exact(gather, chosen(starts_first))
    own_faces = exact(gather[:16], chosen(first))
    faces_out[0] = own_faces[:8]
    faces_out[1] = own_faces[8:]

    pl.semaphore_wait(
        barrier,
        2 + neighbours + is_hub.astype(jnp.int32) * (2 * n_gy - 2 + n_gy * neighbours),
    )

    def input_copy(k):
        return pltpu.make_async_remote_copy(
            src_ref=packs.at[k], dst_ref=inputs.at[k, gy], send_sem=in_send.at[k],
            recv_sem=in_recv.at[k, gy], device_id={"gy": hub}, device_id_type=MESH,
        )

    def face_copy(side):
        return pltpu.make_async_remote_copy(
            src_ref=faces_out.at[side], dst_ref=faces_in.at[1 - side, gy],
            send_sem=f_send.at[side], recv_sem=f_recv.at[1 - side, gy],
            device_id={"gx": sides[side][1], "ta": before, "gy": hub_before},
            device_id_type=MESH,
        )

    def end_copy(p):
        return pltpu.make_async_remote_copy(
            src_ref=field.at[SMAX % 2, p], dst_ref=ends_in, send_sem=e_send.at[p],
            recv_sem=e_recv, device_id={"ta": after, "gy": p}, device_id_type=MESH,
        )

    def robin_copy(side, p):
        return pltpu.make_async_remote_copy(
            src_ref=robin_out.at[side, p], dst_ref=robin_in.at[1 - side],
            send_sem=r_send.at[side, p], recv_sem=r_recv.at[1 - side],
            device_id={"gx": sides[side][1], "ta": after, "gy": p}, device_id_type=MESH,
        )

    @pl.when(jnp.logical_not(is_hub))
    def _():
        for k in range(3):
            input_copy(k).start()

    for side in range(2):
        pl.when(sides[side][0])(face_copy(side).start)

    @pl.when(is_hub)
    def _():
        for k in range(3):
            inputs[k, gy] = packs[k]
        weight, face = weight_ref[...], face_ref[...]

        def wait_inputs(k, p):
            def arrival():
                pltpu.make_async_copy(packs.at[k], inputs.at[k, p], in_recv.at[k, p]).wait()

            pl.when(gy != p)(arrival)

        for p in range(n_gy):
            wait_inputs(0, p)
            kappa = inputs[0, p]
            spread_out = product(spread_ref[...], extended(kappa))
            for b in range(5):
                flux_x[p, :, plane(b)] = spread_out[:, plane(b)] * wy[b]
                flux_y[p, :, plane(b)] = kappa[:, plane(b)] * weight * float(quad[b])
        for p in range(n_gy):
            wait_inputs(1, p)
            for b in range(5):
                inv[p, :, plane(b)] = (step_len / wy[b]) / (inputs[1, p, :, plane(b)] * weight)
        for p in range(n_gy):
            wait_inputs(2, p)
            field[0, p] = inputs[2, p]
            field[1, p] = inputs[2, p]
            drive[p] = jnp.zeros(drive.shape[1:], jnp.float32)

        sections = sec_ref[0]

        def coefficient(j, k):
            value = table_ref[0, 3 * j + k]
            for s in range(1, SMAX - SMIN + 1):
                value = jnp.where(sections == SMIN + s, table_ref[s, 3 * j + k], value)
            return value

        def combine(terms):
            total = terms[0]
            for term in terms[1:]:
                total = total + term
            return total

        def stage(j, carry):
            now = lax.rem(j, 2)
            later = 1 - now
            mu, nu, tilde = (coefficient(j, k) for k in range(3))
            for p in range(n_gy):
                behind = (p + 1) % n_gy
                u = [field[now, p, :, plane(b)] for b in range(5)]
                u.append(field[now, behind, :, plane(0)])
                weights = [flux_y[p, :, plane(b)] for b in range(5)]
                weights.append(flux_y[behind, :, plane(0)])
                flux = [
                    weights[a] * combine([deriv[a][b] * u[b] for b in range(6)])
                    for a in range(6)
                ]
                for b in range(6):
                    value = combine([deriv[a][b] * flux[a] for a in range(6)])
                    if b < 5:
                        y_terms[p, :, plane(b)] = value
                    else:
                        spill[p] = value
            for p in range(n_gy):
                whole = field[now, p]
                count = whole.shape[0]
                slopes = product(slope_ref[...], extended(whole))
                back = product(back_ref[...], slopes * flux_x[p])
                wrapped = rolled(back[count:], 1)
                for b in range(5):
                    u = field[now, p, :, plane(b)]
                    value = back[:count, plane(b)] + y_terms[p, :, plane(b)]
                    if b == 0:
                        value = value + spill[(p - 1) % n_gy]
                    lead = value[:LEAD] + wrapped[:, plane(b)]
                    top = lead[:16] + face * (robin_gain * wy[b]) * u[:16]
                    top = top - drive[p, :, plane(b)]
                    total = jnp.concatenate([top, lead[16:], value[LEAD:]], axis=0)
                    field[later, p, :, plane(b)] = (
                        mu * u
                        + nu * field[later, p, :, plane(b)]
                        - tilde * (inv[p, :, plane(b)] * total)
                    )
            return carry

        lax.fori_loop(0, SMAX, stage, 0)

        for side in range(2):
            there = sides[side][0]

            @pl.when(there)
            def _():
                for p in range(n_gy):
                    pltpu.make_async_copy(
                        faces_out.at[side], faces_in.at[side, p], f_recv.at[side, p]
                    ).wait()
                    hist[side, p] = (2.0 * robin_gain) * faces_in[side, p]

            @pl.when(jnp.logical_not(there))
            def _():
                hist[side] = jnp.zeros(hist.shape[1:], jnp.float32)

        @pl.when(ta == n_ta - 1)
        def _():
            field[0] = inputs[2]

        for p in range(n_gy):
            field[1, p] = field[0, p]
            for side in range(2):
                rows = slice(8 * side, 8 * side + 8)
                known = hist[side, p]
                robin_out[side, p] = (2.0 * robin_gain) * field[0, p, rows] - known
                for b in range(5):
                    drive[p, rows, plane(b)] = face[rows] * wy[b] * known[:, plane(b)]
        for side in range(2):
            @pl.when(sides[side][0])
            def _():
                for p in range(n_gy):
                    robin_copy(side, p).start()

        lax.fori_loop(0, SMAX, stage, 0)

        for p in range(n_gy):
            end_copy(p).start()

    @pl.when(jnp.logical_not(is_hub))
    def _():
        for k in range(3):
            input_copy(k).wait_send()

    for side in range(2):
        there = sides[side][0]
        pl.when(there)(face_copy(side).wait_send)

        @pl.when(there)
        def _():
            pltpu.make_async_copy(
                faces_out.at[side], robin_in.at[side], r_recv.at[side]
            ).wait()
            for b in range(5):
                robin_ref[0, side, 0, b] = robin_in[side, 0:5, plane(b)]

        @pl.when(jnp.logical_not(there))
        def _():
            robin_ref[0, side, 0] = jnp.zeros(robin_ref.shape[3:], jnp.float32)

    pltpu.make_async_copy(packs.at[0], ends_in, e_recv).wait()
    wide = exact(scatter_ref[...], ends_in[...])
    for b in range(5):
        end_ref[0, :, b] = wide[:, plane(b)].reshape(px, 8, LANES)[:, :5]

    @pl.when(is_hub)
    def _():
        for side in range(2):
            @pl.when(sides[side][0])
            def _():
                for p in range(n_gy):
                    robin_copy(side, p).wait_send()
        for p in range(n_gy):
            end_copy(p).wait_send()


def solution(mesh):
    sizes = tuple(mesh.shape[name] for name in ("gx", "ta", "gy"))
    n_gy = sizes[2]

    def local(initial_field, opening_guess, conductivity, capacity, section_count):
        px = initial_field.shape[0]
        tables = constants(px)
        count = len(row_order(px))
        slope_rows = tables[0].shape[0]
        wide = 5 * LANES
        f32 = jnp.float32
        vmem = pl.BlockSpec(memory_space=pltpu.VMEM)
        smem = pl.BlockSpec(memory_space=pltpu.SMEM)
        dma = pltpu.SemaphoreType.DMA
        moved = [
            jnp.transpose(a, (1, 2, 0, 3))
            for a in (initial_field, opening_guess[0], conductivity, capacity)
        ]
        ring = (n_gy, count, wide)
        shapes = [
            (2,) + ring, (3,) + ring, ring, (n_gy, slope_rows, wide), ring, ring,
            (n_gy, count, LANES), (3, count, wide), (count, wide),
            (2, 8, wide), (2, n_gy, 8, wide), (2, n_gy, 8, wide), (2, 8, wide),
            (2, n_gy, 8, wide), (n_gy, 16, wide),
        ]
        return pl.pallas_call(
            functools.partial(kernel, sizes, step_size()),
            out_shape=(
                jax.ShapeDtypeStruct(opening_guess.shape, f32),
                jax.ShapeDtypeStruct((1, 2, 1) + initial_field.shape[1:], f32),
            ),
            in_specs=[vmem] * 4 + [smem] + [vmem] * 7 + [smem],
            out_specs=(vmem, vmem),
            scratch_shapes=[pltpu.VMEM(shape, f32) for shape in shapes]
            + [
                dma((3,)), dma((3, n_gy)), dma((2,)), dma((2, n_gy)),
                dma((2, n_gy)), dma((2,)), dma((n_gy,)), dma,
            ],
            compiler_params=pltpu.CompilerParams(
                collective_id=0, has_side_effects=True, vmem_limit_bytes=32 * 1024 * 1024
            ),
        )(*moved, section_count, *[jnp.asarray(t) for t in tables])

    return jax.shard_map(
        local,
        mesh=mesh,
        in_specs=(
            P("gx", "gy", None, None),
            P("ta", "gx", "gy", None, None),
            P("gx", "gy", None, None),
            P("gx", "gy", None, None),
            P("gx"),
        ),
        out_specs=(P("ta", "gx", "gy", None, None), P("gx", None, "ta", "gy", None, None)),
        check_vma=False,
    )
```

```python
import functools
import math

import jax
import jax.numpy as jnp
import ml_dtypes
import numpy as np
from jax import lax
from jax.experimental import pallas as pl
from jax.experimental.pallas import tpu as pltpu
from jax.sharding import PartitionSpec as P

ITERS = 2
SMIN = 3
SMAX = 4
LANES = 128
MESH = pl.DeviceIdType.MESH

robin_gain = 2.0
kappa_top = 2.0
capacity_low = 0.5
damping = 0.05


def gll_tables():
    root_seven = math.sqrt(7.0)
    outer = math.sqrt(1.0 / 3.0 + 2.0 * root_seven / 21.0)
    closer = math.sqrt(1.0 / 3.0 - 2.0 * root_seven / 21.0)
    points = np.array([-1.0, -outer, -closer, closer, outer, 1.0])
    low, high = (14.0 - root_seven) / 30.0, (14.0 + root_seven) / 30.0
    weights = np.array([1.0 / 15.0, low, high, high, low, 1.0 / 15.0])
    products = np.array(
        [np.prod([points[i] - points[k] for k in range(6) if k != i]) for i in range(6)]
    )
    derivative = np.zeros((6, 6))
    for i in range(6):
        for k in range(6):
            if i != k:
                derivative[i, k] = products[i] / (products[k] * (points[i] - points[k]))
    for i in range(6):
        derivative[i, i] = -derivative[i].sum()
    return (points, weights, derivative)


def line_weights(count, closed):
    weights = gll_tables()[1]
    pattern = np.array([weights[i % 5] if i % 5 else 2.0 * weights[0] for i in range(count)])
    if closed:
        pattern[0] = weights[0]
        pattern[-1] = weights[0]
    return pattern


def step_size():
    points, weights, derivative = gll_tables()
    row_sums = np.abs(derivative).sum(axis=1)
    gersh_bound = max(
        float(np.sum(np.abs(derivative[:, i]) * weights * row_sums) / weights[i]) for i in range(6)
    )
    spectral = kappa_top / capacity_low * 3.0 * gersh_bound + robin_gain / (
        capacity_low * weights[0]
    )
    return float(0.8 * 1.93 * SMIN**2 / spectral)


def rkc_table(sections):
    shifted = 1.0 + damping / sections**2
    cheb, derivs = [1.0, shifted], [0.0, 1.0]
    for j in range(2, SMAX + 1):
        cheb.append(2.0 * shifted * cheb[-1] - cheb[-2])
        derivs.append(2.0 * cheb[j - 1] + 2.0 * shifted * derivs[j - 1] - derivs[j - 2])
    spread = cheb[sections] / derivs[sections]
    rows = [(1.0, 0.0, spread / shifted)]
    for j in range(2, SMAX + 1):
        if j <= sections:
            rows.append(
                (
                    2.0 * shifted * cheb[j - 1] / cheb[j],
                    -cheb[j - 2] / cheb[j],
                    2.0 * spread * cheb[j - 1] / cheb[j],
                )
            )
        else:
            rows.append((1.0, 0.0, 0.0))
    return np.array(rows)


def stacked(matrix):
    matrix = matrix.astype(np.float32)
    high = matrix.astype(ml_dtypes.bfloat16)
    low = (matrix - high.astype(np.float32)).astype(ml_dtypes.bfloat16)
    return np.concatenate([high, high, low], axis=1)


def row_order(px):
    inner = list(range(1, px - 1))
    first, second, third = inner[:3], inner[3:6], inner[6:]
    rows = [(0, q) for q in range(5)] + [(x, 0) for x in first]
    rows += [(px - 1, q) for q in range(5)] + [(x, 0) for x in second]
    rows += [(x, 0) for x in third]
    rows += [(x, q) for x in inner for q in range(1, 5)]
    while len(rows) % 8:
        rows.append((1, 1))
    return rows


LEAD = 24


def constants(px):
    points, quad, deriv = gll_tables()
    wx, wz = line_weights(px, True), line_weights(5, False)
    rows = row_order(px)
    count = len(rows)
    place = {}
    for r, node in enumerate(rows):
        place.setdefault(node, r)
    elements = (px - 1) // 5
    slope_rows = elements * 30 + px * 6
    padded = -(-slope_rows // 16) * 16
    slope = np.zeros((padded, count + LEAD))
    spread = np.zeros((padded, count + LEAD))
    r = 0
    for e in range(elements):
        for a in range(6):
            for q in range(5):
                for b in range(6):
                    slope[r, place[5 * e + b, q]] = deriv[a, b]
                spread[r, place[5 * e + a, q]] = quad[a] * wz[q]
                r += 1
    for x in range(px):
        for a in range(6):
            for b in range(5):
                slope[r, place[x, b]] = deriv[a, b]
            slope[r, count + place[x, 0]] = deriv[a, 5]
            source = place[x, a] if a < 5 else count + place[x, 0]
            spread[r, source] = quad[a] * wx[x]
            r += 1
    high = -(-px // 8) * 8
    gather = np.zeros((count, 5 * high), np.float32)
    scatter = np.zeros((px * 8, count), np.float32)
    for r, (x, q) in enumerate(rows):
        gather[r, high * q + x] = 1.0
    for (x, q), r in place.items():
        scatter[8 * x + q, r] = 1.0
    ones = np.ones((1, LANES))
    weight = np.array([wx[x] * wz[q] for x, q in rows])[:, None] * ones
    face = np.zeros((16, 1))
    face[0:5, 0] = wz
    face[8:13, 0] = wz
    f32 = np.float32
    return (
        np.stack([stacked(slope), stacked(spread)]).astype(f32),
        stacked(slope.T).astype(f32),
        gather,
        scatter,
        weight.astype(f32),
        (face * ones).astype(f32),
    )


def halves(value):
    high = value.astype(jnp.bfloat16)
    low = (value - high.astype(jnp.float32)).astype(jnp.bfloat16)
    return jnp.concatenate([high, low, high], axis=0)


def product(matrix, value):
    return jnp.dot(matrix, halves(value), preferred_element_type=jnp.float32)


def exact(matrix, value):
    return jnp.dot(
        matrix, value, preferred_element_type=jnp.float32, precision=lax.Precision.HIGHEST
    )


def plane(b):
    return slice(LANES * b, LANES * (b + 1))


def rolled(value, shift):
    parts = value.shape[1] // LANES
    return jnp.concatenate(
        [pltpu.roll(value[:, plane(b)], shift % LANES, 1) for b in range(parts)], axis=1
    )


def extended(value):
    return jnp.concatenate([value, rolled(value[:LEAD], -1)], axis=0)


def wide_rows(ref):
    px = ref.shape[2]
    extra = -px % 8
    zeros = jnp.zeros((5, extra, LANES), jnp.float32)
    return [
        jnp.concatenate([ref[b], zeros], axis=1).reshape(5 * (px + extra), LANES)
        for b in range(5)
    ]


def kernel(
    sizes,
    step_len,
    init_hbm, guess_hbm, cond_hbm, cap_hbm, sec_ref,
    forward_hbm, back_hbm, gather_hbm, scatter_hbm, weight_hbm, face_hbm,
    end_ref, robin_ref,
    init_ref, guess_ref, cond_ref, cap_ref,
    forward_ref, back_ref, gather_ref, scatter_ref, weight_ref, face_ref, load_sem,
    field, inputs, inv, flux_x, flux_y, y_terms, spill, packs, ends_in,
    faces_out, faces_in, robin_out, robin_in, hist, drive,
    in_send, in_recv, f_send, f_recv, r_send, r_recv, e_send, e_recv,
):
    n_gx, n_ta, n_gy = sizes
    quad, deriv = gll_tables()[1:]
    plus = [[float(deriv[a, b] + deriv[a, 5 - b]) / 2.0 for b in range(3)] for a in range(3)]
    minus = [[float(deriv[a, b] - deriv[a, 5 - b]) / 2.0 for b in range(3)] for a in range(3)]
    wy = [float(2.0 * quad[0])] + [float(quad[b]) for b in range(1, 5)]
    gx, ta, gy = lax.axis_index("gx"), lax.axis_index("ta"), lax.axis_index("gy")
    after, before = lax.rem(ta + 1, n_ta), lax.rem(ta + n_ta - 1, n_ta)
    low_hub, hubs = (n_gy - 1) // 2, 1 if n_gy == 1 else 2

    def hub_of(block):
        return low_hub + lax.rem(block, hubs)

    hub, hub_before = hub_of(ta), hub_of(before)
    is_hub = gy == hub
    sides = ((gx > 0, gx - 1), (gx < n_gx - 1, gx + 1))
    px = init_ref.shape[2]

    loads = {}
    pairs = (
        (cond_hbm, cond_ref), (gather_hbm, gather_ref), (init_hbm, init_ref),
        (guess_hbm, guess_ref), (cap_hbm, cap_ref), (forward_hbm, forward_ref),
        (back_hbm, back_ref), (scatter_hbm, scatter_ref), (weight_hbm, weight_ref),
        (face_hbm, face_ref),
    )
    for k, (source, target) in enumerate(pairs):
        loads[k] = pltpu.make_async_copy(source, target, load_sem.at[k])

    for load in loads.values():
        load.start()
    barrier = pltpu.get_barrier_semaphore()

    def greet(x, t, y):
        pl.semaphore_signal(
            barrier, inc=1, device_id={"gx": x, "ta": t, "gy": y}, device_id_type=MESH
        )

    neighbours = sides[0][0].astype(jnp.int32) + sides[1][0].astype(jnp.int32)
    greet(gx, before, hub_before)
    for there, x in sides:
        pl.when(there)(functools.partial(greet, x, before, hub_before))
    pl.when(jnp.logical_not(is_hub))(functools.partial(greet, gx, ta, hub))

    @pl.when(is_hub)
    def _():
        for p in range(n_gy):
            pl.when(gy != p)(functools.partial(greet, gx, ta, p))
            greet(gx, after, p)
            for there, x in sides:
                pl.when(there)(functools.partial(greet, x, after, p))

    for k in (1, 2, 3):
        loads[k].wait()
    gather = gather_ref[...]
    first = ta == 0
    starts_first = jnp.logical_or(first, ta == n_ta - 1)
    fresh, guess = wide_rows(init_ref), wide_rows(guess_ref)

    def chosen(there):
        return jnp.concatenate(
            [jnp.where(there, fresh[b], guess[b]) for b in range(5)], axis=1
        )

    loads[0].wait()
    packs[0] = exact(gather, jnp.concatenate(wide_rows(cond_ref), axis=1))
    packs[1] = exact(gather, chosen(starts_first))
    loads[4].wait()
    packs[2] = exact(gather, jnp.concatenate(wide_rows(cap_ref), axis=1))
    for k in range(5, len(pairs)):
        loads[k].wait()
    own_faces = exact(gather[:16], chosen(first))
    faces_out[0] = own_faces[:8]
    faces_out[1] = own_faces[8:]

    pl.semaphore_wait(
        barrier,
        2 + neighbours + is_hub.astype(jnp.int32) * (2 * n_gy - 2 + n_gy * neighbours),
    )

    def input_copy(k):
        return pltpu.make_async_remote_copy(
            src_ref=packs.at[k], dst_ref=inputs.at[k, gy], send_sem=in_send.at[k],
            recv_sem=in_recv.at[k, gy], device_id={"gy": hub}, device_id_type=MESH,
        )

    def face_copy(side):
        return pltpu.make_async_remote_copy(
            src_ref=faces_out.at[side], dst_ref=faces_in.at[1 - side, gy],
            send_sem=f_send.at[side], recv_sem=f_recv.at[1 - side, gy],
            device_id={"gx": sides[side][1], "ta": before, "gy": hub_before},
            device_id_type=MESH,
        )

    def end_copy(p):
        return pltpu.make_async_remote_copy(
            src_ref=field.at[SMAX % 2, p], dst_ref=ends_in, send_sem=e_send.at[p],
            recv_sem=e_recv, device_id={"ta": after, "gy": p}, device_id_type=MESH,
        )

    def robin_copy(side, p):
        return pltpu.make_async_remote_copy(
            src_ref=robin_out.at[side, p], dst_ref=robin_in.at[1 - side],
            send_sem=r_send.at[side, p], recv_sem=r_recv.at[1 - side],
            device_id={"gx": sides[side][1], "ta": after, "gy": p}, device_id_type=MESH,
        )

    @pl.when(jnp.logical_not(is_hub))
    def _():
        for k in range(3):
            input_copy(k).start()

    for side in range(2):
        pl.when(sides[side][0])(face_copy(side).start)

    @pl.when(is_hub)
    def _():
        for k in range(3):
            inputs[k, gy] = packs[k]
        weight, face = weight_ref[...], face_ref[...]

        def wait_inputs(k, p):
            def arrival():
                pltpu.make_async_copy(packs.at[k], inputs.at[k, p], in_recv.at[k, p]).wait()

            pl.when(gy != p)(arrival)

        for p in range(n_gy):
            wait_inputs(0, p)
            kappa = inputs[0, p]
            spread_out = product(forward_ref[1].astype(jnp.bfloat16), extended(kappa))
            for b in range(5):
                flux_x[p, :, plane(b)] = spread_out[:, plane(b)] * wy[b]
                flux_y[p, :, plane(b)] = kappa[:, plane(b)] * weight * float(quad[b])
        for p in range(n_gy):
            wait_inputs(1, p)
            field[0, p] = inputs[1, p]
            field[1, p] = inputs[1, p]
            drive[p] = jnp.zeros(drive.shape[1:], jnp.float32)

        def set_inverse(p):
            wait_inputs(2, p)
            for b in range(5):
                inv[p, :, plane(b)] = (step_len / wy[b]) / (inputs[2, p, :, plane(b)] * weight)

        sections = sec_ref[0]

        def coefficient(j, k):
            value = jnp.float32(0.0)
            for count in range(SMIN, SMAX + 1):
                for at, row in enumerate(rkc_table(count)):
                    here = jnp.logical_and(sections == count, j == at)
                    value = jnp.where(here, jnp.float32(row[k]), value)
            return value

        def combine(terms):
            total = terms[0]
            for term in terms[1:]:
                total = total + term
            return total

        def stage(j, carry, ready=None, done=None):
            now = j % 2
            later = 1 - now
            forward = forward_ref[0].astype(jnp.bfloat16)
            backward = back_ref[...].astype(jnp.bfloat16)
            mu, nu, tilde = (coefficient(j, k) for k in range(3))
            for p in range(n_gy):
                behind = (p + 1) % n_gy
                u = [field[now, p, :, plane(b)] for b in range(5)]
                u.append(field[now, behind, :, plane(0)])
                weights = [flux_y[p, :, plane(b)] for b in range(5)]
                weights.append(flux_y[behind, :, plane(0)])
                sums = [u[b] + u[5 - b] for b in range(3)]
                gaps = [u[b] - u[5 - b] for b in range(3)]
                even = [combine([plus[a][b] * sums[b] for b in range(3)]) for a in range(3)]
                odd = [combine([minus[a][b] * gaps[b] for b in range(3)]) for a in range(3)]
                low = [weights[a] * (odd[a] + even[a]) for a in range(3)]
                high = [weights[5 - a] * (odd[a] - even[a]) for a in range(3)]
                sums = [low[a] + high[a] for a in range(3)]
                gaps = [low[a] - high[a] for a in range(3)]
                even = [combine([plus[a][b] * gaps[a] for a in range(3)]) for b in range(3)]
                odd = [combine([minus[a][b] * sums[a] for a in range(3)]) for b in range(3)]
                for b in range(6):
                    value = even[b] + odd[b] if b < 3 else even[5 - b] - odd[5 - b]
                    if b < 5:
                        y_terms[p, :, plane(b)] = value
                    else:
                        spill[p] = value
            for p in range(n_gy):
                if ready is not None:
                    ready(p)
                whole = field[now, p]
                count = whole.shape[0]
                slopes = product(forward, extended(whole))
                back = product(backward, slopes * flux_x[p])
                wrapped = rolled(back[count:], 1)
                for b in range(5):
                    u = field[now, p, :, plane(b)]
                    value = back[:count, plane(b)] + y_terms[p, :, plane(b)]
                    if b == 0:
                        value = value + spill[(p - 1) % n_gy]
                    lead = value[:LEAD] + wrapped[:, plane(b)]
                    top = lead[:16] + face * (robin_gain * wy[b]) * u[:16]
                    top = top - drive[p, :, plane(b)]
                    total = jnp.concatenate([top, lead[16:], value[LEAD:]], axis=0)
                    field[later, p, :, plane(b)] = (
                        mu * u
                        + nu * field[later, p, :, plane(b)]
                        - tilde * (inv[p, :, plane(b)] * total)
                    )
                if done is not None:
                    done(p)
            return carry

        stage(0, 0, ready=set_inverse)
        lax.fori_loop(1, SMAX, stage, 0)

        for side in range(2):
            there = sides[side][0]

            @pl.when(there)
            def _():
                for p in range(n_gy):
                    pltpu.make_async_copy(
                        faces_out.at[side], faces_in.at[side, p], f_recv.at[side, p]
                    ).wait()
                    hist[side, p] = (2.0 * robin_gain) * faces_in[side, p]

            @pl.when(jnp.logical_not(there))
            def _():
                hist[side] = jnp.zeros(hist.shape[1:], jnp.float32)

        @pl.when(ta == n_ta - 1)
        def _():
            field[0] = inputs[1]

        for p in range(n_gy):
            field[1, p] = field[0, p]
            for side in range(2):
                rows = slice(8 * side, 8 * side + 8)
                known = hist[side, p]
                robin_out[side, p] = (2.0 * robin_gain) * field[0, p, rows] - known
                for b in range(5):
                    drive[p, rows, plane(b)] = face[rows] * wy[b] * known[:, plane(b)]
        for side in range(2):
            @pl.when(sides[side][0])
            def _():
                for p in range(n_gy):
                    robin_copy(side, p).start()

        lax.fori_loop(0, SMAX - 1, stage, 0)
        stage(SMAX - 1, 0, done=lambda p: end_copy(p).start())

    @pl.when(jnp.logical_not(is_hub))
    def _():
        for k in range(3):
            input_copy(k).wait_send()

    for side in range(2):
        there = sides[side][0]
        pl.when(there)(face_copy(side).wait_send)

        @pl.when(there)
        def _():
            pltpu.make_async_copy(
                faces_out.at[side], robin_in.at[side], r_recv.at[side]
            ).wait()
            for b in range(5):
                robin_ref[0, side, 0, b] = robin_in[side, 0:5, plane(b)]

        @pl.when(jnp.logical_not(there))
        def _():
            robin_ref[0, side, 0] = jnp.zeros(robin_ref.shape[3:], jnp.float32)

    pltpu.make_async_copy(packs.at[0], ends_in, e_recv).wait()
    wide = exact(scatter_ref[...], ends_in[...])
    for b in range(5):
        end_ref[0, :, b] = wide[:, plane(b)].reshape(px, 8, LANES)[:, :5]

    @pl.when(is_hub)
    def _():
        for side in range(2):
            @pl.when(sides[side][0])
            def _():
                for p in range(n_gy):
                    robin_copy(side, p).wait_send()
        for p in range(n_gy):
            end_copy(p).wait_send()


def solution(mesh):
    sizes = tuple(mesh.shape[name] for name in ("gx", "ta", "gy"))
    n_gy = sizes[2]

    def local(initial_field, opening_guess, conductivity, capacity, section_count):
        px = initial_field.shape[0]
        tables = constants(px)
        count = len(row_order(px))
        slope_rows = tables[0].shape[1]
        wide = 5 * LANES
        f32 = jnp.float32
        vmem = pl.BlockSpec(memory_space=pltpu.VMEM)
        smem = pl.BlockSpec(memory_space=pltpu.SMEM)
        hbm = pl.BlockSpec(memory_space=pltpu.HBM)
        dma = pltpu.SemaphoreType.DMA
        moved = [
            jnp.transpose(a, (1, 2, 0, 3))
            for a in (initial_field, opening_guess[0], conductivity, capacity)
        ]
        ring = (n_gy, count, wide)
        shapes = [
            (2,) + ring, (3,) + ring, ring, (n_gy, slope_rows, wide), ring, ring,
            (n_gy, count, LANES), (3, count, wide), (count, wide),
            (2, 8, wide), (2, n_gy, 8, wide), (2, n_gy, 8, wide), (2, 8, wide),
            (2, n_gy, 8, wide), (n_gy, 16, wide),
        ]
        return pl.pallas_call(
            functools.partial(kernel, sizes, step_size()),
            out_shape=(
                jax.ShapeDtypeStruct(opening_guess.shape, f32),
                jax.ShapeDtypeStruct((1, 2, 1) + initial_field.shape[1:], f32),
            ),
            in_specs=[hbm] * 4 + [smem] + [hbm] * len(tables),
            out_specs=(vmem, vmem),
            scratch_shapes=[pltpu.VMEM(a.shape, f32) for a in moved]
            + [pltpu.VMEM(t.shape, t.dtype) for t in tables]
            + [dma((4 + len(tables),))]
            + [pltpu.VMEM(shape, f32) for shape in shapes]
            + [
                dma((3,)), dma((3, n_gy)), dma((2,)), dma((2, n_gy)),
                dma((2, n_gy)), dma((2,)), dma((n_gy,)), dma,
            ],
            compiler_params=pltpu.CompilerParams(
                collective_id=0, has_side_effects=True, vmem_limit_bytes=63 * 1024 * 1024
            ),
        )(*moved, section_count, *[jnp.asarray(t) for t in tables])

    return jax.shard_map(
        local,
        mesh=mesh,
        in_specs=(
            P("gx", "gy", None, None),
            P("ta", "gx", "gy", None, None),
            P("gx", "gy", None, None),
            P("gx", "gy", None, None),
            P("gx"),
        ),
        out_specs=(P("ta", "gx", "gy", None, None), P("gx", None, "ta", "gy", None, None)),
        check_vma=False,
    )
```

```python
import functools
import math

import jax
import jax.numpy as jnp
import ml_dtypes
import numpy as np
from jax import lax
from jax.experimental import pallas as pl
from jax.experimental.pallas import tpu as pltpu
from jax.sharding import PartitionSpec as P

ITERS = 2
SMIN = 3
SMAX = 4
LANES = 128
MESH = pl.DeviceIdType.MESH

robin_gain = 2.0
kappa_top = 2.0
capacity_low = 0.5
damping = 0.05


def gll_tables():
    root_seven = math.sqrt(7.0)
    outer = math.sqrt(1.0 / 3.0 + 2.0 * root_seven / 21.0)
    closer = math.sqrt(1.0 / 3.0 - 2.0 * root_seven / 21.0)
    points = np.array([-1.0, -outer, -closer, closer, outer, 1.0])
    low, high = (14.0 - root_seven) / 30.0, (14.0 + root_seven) / 30.0
    weights = np.array([1.0 / 15.0, low, high, high, low, 1.0 / 15.0])
    products = np.array(
        [np.prod([points[i] - points[k] for k in range(6) if k != i]) for i in range(6)]
    )
    derivative = np.zeros((6, 6))
    for i in range(6):
        for k in range(6):
            if i != k:
                derivative[i, k] = products[i] / (products[k] * (points[i] - points[k]))
    for i in range(6):
        derivative[i, i] = -derivative[i].sum()
    return (points, weights, derivative)


def line_weights(count, closed):
    weights = gll_tables()[1]
    pattern = np.array([weights[i % 5] if i % 5 else 2.0 * weights[0] for i in range(count)])
    if closed:
        pattern[0] = weights[0]
        pattern[-1] = weights[0]
    return pattern


def step_size():
    points, weights, derivative = gll_tables()
    row_sums = np.abs(derivative).sum(axis=1)
    gersh_bound = max(
        float(np.sum(np.abs(derivative[:, i]) * weights * row_sums) / weights[i]) for i in range(6)
    )
    spectral = kappa_top / capacity_low * 3.0 * gersh_bound + robin_gain / (
        capacity_low * weights[0]
    )
    return float(0.8 * 1.93 * SMIN**2 / spectral)


def rkc_table(sections):
    shifted = 1.0 + damping / sections**2
    cheb, derivs = [1.0, shifted], [0.0, 1.0]
    for j in range(2, SMAX + 1):
        cheb.append(2.0 * shifted * cheb[-1] - cheb[-2])
        derivs.append(2.0 * cheb[j - 1] + 2.0 * shifted * derivs[j - 1] - derivs[j - 2])
    spread = cheb[sections] / derivs[sections]
    rows = [(1.0, 0.0, spread / shifted)]
    for j in range(2, SMAX + 1):
        if j <= sections:
            rows.append(
                (
                    2.0 * shifted * cheb[j - 1] / cheb[j],
                    -cheb[j - 2] / cheb[j],
                    2.0 * spread * cheb[j - 1] / cheb[j],
                )
            )
        else:
            rows.append((1.0, 0.0, 0.0))
    return np.array(rows)


def stacked(matrix):
    matrix = matrix.astype(np.float32)
    high = matrix.astype(ml_dtypes.bfloat16)
    low = (matrix - high.astype(np.float32)).astype(ml_dtypes.bfloat16)
    return np.concatenate([high, high, low], axis=1)


def row_order(px):
    inner = list(range(1, px - 1))
    first, second, third = inner[:3], inner[3:6], inner[6:]
    rows = [(0, q) for q in range(5)] + [(x, 0) for x in first]
    rows += [(px - 1, q) for q in range(5)] + [(x, 0) for x in second]
    rows += [(x, 0) for x in third]
    rows += [(x, q) for x in inner for q in range(1, 5)]
    while len(rows) % 8:
        rows.append((1, 1))
    return rows


LEAD = 24


def constants(px):
    points, quad, deriv = gll_tables()
    wx, wz = line_weights(px, True), line_weights(5, False)
    rows = row_order(px)
    count = len(rows)
    place = {}
    for r, node in enumerate(rows):
        place.setdefault(node, r)
    elements = (px - 1) // 5
    slope_rows = elements * 30 + px * 6
    padded = -(-slope_rows // 16) * 16
    slope = np.zeros((padded, count + LEAD))
    spread = np.zeros((padded, count + LEAD))
    r = 0
    for e in range(elements):
        for a in range(6):
            for q in range(5):
                for b in range(6):
                    slope[r, place[5 * e + b, q]] = deriv[a, b]
                spread[r, place[5 * e + a, q]] = quad[a] * wz[q]
                r += 1
    for x in range(px):
        for a in range(6):
            for b in range(5):
                slope[r, place[x, b]] = deriv[a, b]
            slope[r, count + place[x, 0]] = deriv[a, 5]
            source = place[x, a] if a < 5 else count + place[x, 0]
            spread[r, source] = quad[a] * wx[x]
            r += 1
    high = -(-px // 8) * 8
    gather = np.zeros((count, 5 * high), np.float32)
    scatter = np.zeros((px * 8, count), np.float32)
    for r, (x, q) in enumerate(rows):
        gather[r, high * q + x] = 1.0
    for (x, q), r in place.items():
        scatter[8 * x + q, r] = 1.0
    ones = np.ones((1, LANES))
    weight = np.array([wx[x] * wz[q] for x, q in rows])[:, None] * ones
    face = np.zeros((16, 1))
    face[0:5, 0] = wz
    face[8:13, 0] = wz
    f32 = np.float32
    return (
        np.stack([stacked(slope), stacked(spread)]).astype(f32),
        stacked(slope.T).astype(f32),
        gather,
        scatter,
        weight.astype(f32),
        (face * ones).astype(f32),
    )


def halves(value):
    high = value.astype(jnp.bfloat16)
    low = (value - high.astype(jnp.float32)).astype(jnp.bfloat16)
    return jnp.concatenate([high, low, high], axis=0)


def product(matrix, value):
    return jnp.dot(matrix, halves(value), preferred_element_type=jnp.float32)


def exact(matrix, value):
    return jnp.dot(
        matrix, value, preferred_element_type=jnp.float32, precision=lax.Precision.HIGHEST
    )


def plane(b):
    return slice(LANES * b, LANES * (b + 1))


def rolled(value, shift):
    parts = value.shape[1] // LANES
    return jnp.concatenate(
        [pltpu.roll(value[:, plane(b)], shift % LANES, 1) for b in range(parts)], axis=1
    )


def extended(value):
    return jnp.concatenate([value, rolled(value[:LEAD], -1)], axis=0)


def wide_rows(ref):
    px = ref.shape[2]
    extra = -px % 8
    zeros = jnp.zeros((5, extra, LANES), jnp.float32)
    return [
        jnp.concatenate([ref[b], zeros], axis=1).reshape(5 * (px + extra), LANES)
        for b in range(5)
    ]


def kernel(
    sizes,
    step_len,
    init_hbm, guess_hbm, cond_hbm, cap_hbm, sec_ref,
    forward_hbm, back_hbm, gather_hbm, scatter_hbm, weight_hbm, face_hbm,
    end_ref, robin_ref,
    init_ref, guess_ref, cond_ref, cap_ref,
    forward_ref, back_ref, gather_ref, scatter_ref, weight_ref, face_ref, load_sem,
    field, inputs, inv, flux_x, flux_y, y_terms, spill, packs, ends_in,
    faces_out, faces_in, robin_out, robin_in, hist, drive,
    in_send, in_recv, f_send, f_recv, r_send, r_recv, e_send, e_recv,
):
    n_gx, n_ta, n_gy = sizes
    quad, deriv = gll_tables()[1:]
    plus = [[float(deriv[a, b] + deriv[a, 5 - b]) / 2.0 for b in range(3)] for a in range(3)]
    minus = [[float(deriv[a, b] - deriv[a, 5 - b]) / 2.0 for b in range(3)] for a in range(3)]
    wy = [float(2.0 * quad[0])] + [float(quad[b]) for b in range(1, 5)]
    gx, ta, gy = lax.axis_index("gx"), lax.axis_index("ta"), lax.axis_index("gy")
    after, before = lax.rem(ta + 1, n_ta), lax.rem(ta + n_ta - 1, n_ta)
    low_hub, hubs = (n_gy - 1) // 2, 1 if n_gy == 1 else 2

    def hub_of(block):
        return low_hub + lax.rem(block, hubs)

    hub, hub_before = hub_of(ta), hub_of(before)
    is_hub = gy == hub
    sides = ((gx > 0, gx - 1), (gx < n_gx - 1, gx + 1))
    px = init_ref.shape[2]

    loads = {}
    pairs = (
        (cond_hbm, cond_ref), (gather_hbm, gather_ref), (init_hbm, init_ref),
        (guess_hbm, guess_ref), (cap_hbm, cap_ref), (forward_hbm, forward_ref),
        (back_hbm, back_ref), (scatter_hbm, scatter_ref), (weight_hbm, weight_ref),
        (face_hbm, face_ref),
    )
    for k, (source, target) in enumerate(pairs):
        loads[k] = pltpu.make_async_copy(source, target, load_sem.at[k])

    for load in loads.values():
        load.start()
    barrier = pltpu.get_barrier_semaphore()

    def greet(x, t, y):
        pl.semaphore_signal(
            barrier, inc=1, device_id={"gx": x, "ta": t, "gy": y}, device_id_type=MESH
        )

    neighbours = sides[0][0].astype(jnp.int32) + sides[1][0].astype(jnp.int32)
    greet(gx, before, hub_before)
    for there, x in sides:
        pl.when(there)(functools.partial(greet, x, before, hub_before))
    pl.when(jnp.logical_not(is_hub))(functools.partial(greet, gx, ta, hub))

    @pl.when(is_hub)
    def _():
        for p in range(n_gy):
            pl.when(gy != p)(functools.partial(greet, gx, ta, p))
            greet(gx, after, p)
            for there, x in sides:
                pl.when(there)(functools.partial(greet, x, after, p))

    for k in (1, 2, 3):
        loads[k].wait()
    gather = gather_ref[...]
    first = ta == 0
    starts_first = jnp.logical_or(first, ta == n_ta - 1)
    fresh, guess = wide_rows(init_ref), wide_rows(guess_ref)

    def chosen(there):
        return jnp.concatenate(
            [jnp.where(there, fresh[b], guess[b]) for b in range(5)], axis=1
        )

    loads[0].wait()
    packs[0] = exact(gather, jnp.concatenate(wide_rows(cond_ref), axis=1))
    pl.semaphore_wait(
        barrier,
        2 + neighbours + is_hub.astype(jnp.int32) * (2 * n_gy - 2 + n_gy * neighbours),
    )

    def input_copy(k):
        return pltpu.make_async_remote_copy(
            src_ref=packs.at[k], dst_ref=inputs.at[k, gy], send_sem=in_send.at[k],
            recv_sem=in_recv.at[k, gy], device_id={"gy": hub}, device_id_type=MESH,
        )

    def face_copy(side):
        return pltpu.make_async_remote_copy(
            src_ref=faces_out.at[side], dst_ref=faces_in.at[1 - side, gy],
            send_sem=f_send.at[side], recv_sem=f_recv.at[1 - side, gy],
            device_id={"gx": sides[side][1], "ta": before, "gy": hub_before},
            device_id_type=MESH,
        )

    def end_copy(p):
        return pltpu.make_async_remote_copy(
            src_ref=field.at[SMAX % 2, p], dst_ref=ends_in, send_sem=e_send.at[p],
            recv_sem=e_recv, device_id={"ta": after, "gy": p}, device_id_type=MESH,
        )

    def robin_copy(side, p):
        return pltpu.make_async_remote_copy(
            src_ref=robin_out.at[side, p], dst_ref=robin_in.at[1 - side],
            send_sem=r_send.at[side, p], recv_sem=r_recv.at[1 - side],
            device_id={"gx": sides[side][1], "ta": after, "gy": p}, device_id_type=MESH,
        )

    pl.when(jnp.logical_not(is_hub))(input_copy(0).start)
    packs[1] = exact(gather, chosen(starts_first))
    pl.when(jnp.logical_not(is_hub))(input_copy(1).start)
    loads[4].wait()
    packs[2] = exact(gather, jnp.concatenate(wide_rows(cap_ref), axis=1))
    pl.when(jnp.logical_not(is_hub))(input_copy(2).start)
    for k in range(5, len(pairs)):
        loads[k].wait()
    own_faces = exact(gather[:16], chosen(first))
    faces_out[0] = own_faces[:8]
    faces_out[1] = own_faces[8:]

    for side in range(2):
        pl.when(sides[side][0])(face_copy(side).start)

    @pl.when(is_hub)
    def _():
        for k in range(3):
            inputs[k, gy] = packs[k]
        weight, face = weight_ref[...], face_ref[...]

        def wait_inputs(k, p):
            def arrival():
                pltpu.make_async_copy(packs.at[k], inputs.at[k, p], in_recv.at[k, p]).wait()

            pl.when(gy != p)(arrival)

        for p in range(n_gy):
            wait_inputs(0, p)
            kappa = inputs[0, p]
            spread_out = product(forward_ref[1].astype(jnp.bfloat16), extended(kappa))
            for b in range(5):
                flux_x[p, :, plane(b)] = spread_out[:, plane(b)] * wy[b]
                flux_y[p, :, plane(b)] = kappa[:, plane(b)] * weight * float(quad[b])
        for p in range(n_gy):
            wait_inputs(1, p)
            field[0, p] = inputs[1, p]
            field[1, p] = inputs[1, p]
            drive[p] = jnp.zeros(drive.shape[1:], jnp.float32)

        def set_inverse(p):
            wait_inputs(2, p)
            for b in range(5):
                inv[p, :, plane(b)] = (step_len / wy[b]) / (inputs[2, p, :, plane(b)] * weight)

        sections = sec_ref[0]

        def coefficient(j, k):
            value = jnp.float32(0.0)
            for count in range(SMIN, SMAX + 1):
                for at, row in enumerate(rkc_table(count)):
                    here = jnp.logical_and(sections == count, j == at)
                    value = jnp.where(here, jnp.float32(row[k]), value)
            return value

        def combine(terms):
            total = terms[0]
            for term in terms[1:]:
                total = total + term
            return total

        def stage(j, carry, ready=None, done=None):
            now = j % 2
            later = 1 - now
            forward = forward_ref[0].astype(jnp.bfloat16)
            backward = back_ref[...].astype(jnp.bfloat16)
            mu, nu, tilde = (coefficient(j, k) for k in range(3))
            for p in range(n_gy):
                behind = (p + 1) % n_gy
                u = [field[now, p, :, plane(b)] for b in range(5)]
                u.append(field[now, behind, :, plane(0)])
                weights = [flux_y[p, :, plane(b)] for b in range(5)]
                weights.append(flux_y[behind, :, plane(0)])
                sums = [u[b] + u[5 - b] for b in range(3)]
                gaps = [u[b] - u[5 - b] for b in range(3)]
                even = [combine([plus[a][b] * sums[b] for b in range(3)]) for a in range(3)]
                odd = [combine([minus[a][b] * gaps[b] for b in range(3)]) for a in range(3)]
                low = [weights[a] * (odd[a] + even[a]) for a in range(3)]
                high = [weights[5 - a] * (odd[a] - even[a]) for a in range(3)]
                sums = [low[a] + high[a] for a in range(3)]
                gaps = [low[a] - high[a] for a in range(3)]
                even = [combine([plus[a][b] * gaps[a] for a in range(3)]) for b in range(3)]
                odd = [combine([minus[a][b] * sums[a] for a in range(3)]) for b in range(3)]
                for b in range(6):
                    value = even[b] + odd[b] if b < 3 else even[5 - b] - odd[5 - b]
                    if b < 5:
                        y_terms[p, :, plane(b)] = value
                    else:
                        spill[p] = value
            for p in range(n_gy):
                if ready is not None:
                    ready(p)
                whole = field[now, p]
                count = whole.shape[0]
                slopes = product(forward, extended(whole))
                back = product(backward, slopes * flux_x[p])
                wrapped = rolled(back[count:], 1)
                for b in range(5):
                    u = field[now, p, :, plane(b)]
                    value = back[:count, plane(b)] + y_terms[p, :, plane(b)]
                    if b == 0:
                        value = value + spill[(p - 1) % n_gy]
                    lead = value[:LEAD] + wrapped[:, plane(b)]
                    top = lead[:16] + face * (robin_gain * wy[b]) * u[:16]
                    top = top - drive[p, :, plane(b)]
                    total = jnp.concatenate([top, lead[16:], value[LEAD:]], axis=0)
                    field[later, p, :, plane(b)] = (
                        mu * u
                        + nu * field[later, p, :, plane(b)]
                        - tilde * (inv[p, :, plane(b)] * total)
                    )
                if done is not None:
                    done(p)
            return carry

        stage(0, 0, ready=set_inverse)
        for j in range(1, SMAX):
            stage(j, 0)

        for side in range(2):
            there = sides[side][0]

            @pl.when(there)
            def _():
                for p in range(n_gy):
                    pltpu.make_async_copy(
                        faces_out.at[side], faces_in.at[side, p], f_recv.at[side, p]
                    ).wait()
                    hist[side, p] = (2.0 * robin_gain) * faces_in[side, p]

            @pl.when(jnp.logical_not(there))
            def _():
                hist[side] = jnp.zeros(hist.shape[1:], jnp.float32)

        @pl.when(ta == n_ta - 1)
        def _():
            field[0] = inputs[1]

        for p in range(n_gy):
            field[1, p] = field[0, p]
            for side in range(2):
                rows = slice(8 * side, 8 * side + 8)
                known = hist[side, p]
                robin_out[side, p] = (2.0 * robin_gain) * field[0, p, rows] - known
                for b in range(5):
                    drive[p, rows, plane(b)] = face[rows] * wy[b] * known[:, plane(b)]
        for side in range(2):
            @pl.when(sides[side][0])
            def _():
                for p in range(n_gy):
                    robin_copy(side, p).start()

        for j in range(SMAX - 1):
            stage(j, 0)
        stage(SMAX - 1, 0, done=lambda p: end_copy(p).start())

    @pl.when(jnp.logical_not(is_hub))
    def _():
        for k in range(3):
            input_copy(k).wait_send()

    for side in range(2):
        there = sides[side][0]
        pl.when(there)(face_copy(side).wait_send)

        @pl.when(there)
        def _():
            pltpu.make_async_copy(
                faces_out.at[side], robin_in.at[side], r_recv.at[side]
            ).wait()
            for b in range(5):
                robin_ref[0, side, 0, b] = robin_in[side, 0:5, plane(b)]

        @pl.when(jnp.logical_not(there))
        def _():
            robin_ref[0, side, 0] = jnp.zeros(robin_ref.shape[3:], jnp.float32)

    pltpu.make_async_copy(packs.at[0], ends_in, e_recv).wait()
    wide = exact(scatter_ref[...], ends_in[...])
    for b in range(5):
        end_ref[0, :, b] = wide[:, plane(b)].reshape(px, 8, LANES)[:, :5]

    @pl.when(is_hub)
    def _():
        for side in range(2):
            @pl.when(sides[side][0])
            def _():
                for p in range(n_gy):
                    robin_copy(side, p).wait_send()
        for p in range(n_gy):
            end_copy(p).wait_send()


def solution(mesh):
    sizes = tuple(mesh.shape[name] for name in ("gx", "ta", "gy"))
    n_gy = sizes[2]

    def local(initial_field, opening_guess, conductivity, capacity, section_count):
        px = initial_field.shape[0]
        tables = constants(px)
        count = len(row_order(px))
        slope_rows = tables[0].shape[1]
        wide = 5 * LANES
        f32 = jnp.float32
        vmem = pl.BlockSpec(memory_space=pltpu.VMEM)
        smem = pl.BlockSpec(memory_space=pltpu.SMEM)
        hbm = pl.BlockSpec(memory_space=pltpu.HBM)
        dma = pltpu.SemaphoreType.DMA
        moved = [
            jnp.transpose(a, (1, 2, 0, 3))
            for a in (initial_field, opening_guess[0], conductivity, capacity)
        ]
        ring = (n_gy, count, wide)
        shapes = [
            (2,) + ring, (3,) + ring, ring, (n_gy, slope_rows, wide), ring, ring,
            (n_gy, count, LANES), (3, count, wide), (count, wide),
            (2, 8, wide), (2, n_gy, 8, wide), (2, n_gy, 8, wide), (2, 8, wide),
            (2, n_gy, 8, wide), (n_gy, 16, wide),
        ]
        return pl.pallas_call(
            functools.partial(kernel, sizes, step_size()),
            out_shape=(
                jax.ShapeDtypeStruct(opening_guess.shape, f32),
                jax.ShapeDtypeStruct((1, 2, 1) + initial_field.shape[1:], f32),
            ),
            in_specs=[hbm] * 4 + [smem] + [hbm] * len(tables),
            out_specs=(vmem, vmem),
            scratch_shapes=[pltpu.VMEM(a.shape, f32) for a in moved]
            + [pltpu.VMEM(t.shape, t.dtype) for t in tables]
            + [dma((4 + len(tables),))]
            + [pltpu.VMEM(shape, f32) for shape in shapes]
            + [
                dma((3,)), dma((3, n_gy)), dma((2,)), dma((2, n_gy)),
                dma((2, n_gy)), dma((2,)), dma((n_gy,)), dma,
            ],
            compiler_params=pltpu.CompilerParams(
                collective_id=0, has_side_effects=True, vmem_limit_bytes=63 * 1024 * 1024
            ),
        )(*moved, section_count, *[jnp.asarray(t) for t in tables])

    return jax.shard_map(
        local,
        mesh=mesh,
        in_specs=(
            P("gx", "gy", None, None),
            P("ta", "gx", "gy", None, None),
            P("gx", "gy", None, None),
            P("gx", "gy", None, None),
            P("gx"),
        ),
        out_specs=(P("ta", "gx", "gy", None, None), P("gx", None, "ta", "gy", None, None)),
        check_vma=False,
    )
```
